128 devices in a mesh: grp: 16 (over x_lo, y, core), blk: 8 (over x_hi, z).
Axes of the slice: x: 4 (x_hi: 2, x_lo: 2; x = x_hi * 2 + x_lo), y: 4, z: 4, core: 2. Of those that a mesh axis runs over, the one named last changes fastest.
Arguments:
- embed: bfloat16 [65536, 1024], P(('grp', 'blk')), may hold values from -6 to 6
- dest: int32 [65536], P(('grp', 'blk')), may hold values from 0 to 127, as said below
- slot: int32 [65536], P(('grp', 'blk')), may hold values from 0 to 511, as said below
Outputs:
- best: float32 [65536], P(('grp', 'blk'))
The draws below stay inside these ranges and needn't reach their ends.
Inputs may be any that keep to these rules, and one draw needn't show every extreme that they name: Each device index receives exactly 512 documents; at most 8 documents of one device's rows name the same dest, and in every draw some device sends exactly 8 to some dest. The pairs (dest, slot) are all different.
All inputs are finite; a program needn't handle non-finite values.
Results may differ from the reference program's by a relative error of at most 0.0013.
Values may be sent and summed in bfloat16 or wider, within the bound.
A program may use at most 64 MiB of HBM per device.

```python
import jax
import jax.numpy as jnp
from jax import lax

D = 1024
MEM_DEV = 512
DOCS = 65536
CLUSTER = 4096
N_GRP = 16
N_BLK = 8


def route_plan(key):
    ndev = N_GRP * N_BLK
    base = MEM_DEV // ndev
    half = base // 2
    steps = jnp.arange(ndev, dtype=jnp.int32)
    values = jnp.where(steps % 2 == 0, base - half, base + half).astype(jnp.int32)
    values = values.at[1].set(base + 2 * half).at[3].set(base)
    values = jax.random.permutation(jax.random.fold_in(key, 11), values)
    counts = values[(steps[None, :] - steps[:, None]) % ndev]
    row_start = jnp.cumsum(counts, axis=1) - counts
    row_end = row_start + counts
    col_start = jnp.cumsum(counts, axis=0) - counts
    src_keys = jax.random.split(jax.random.fold_in(key, 12), ndev)
    order = jax.vmap(lambda kk: jax.random.permutation(kk, MEM_DEV))(src_keys).astype(jnp.int32)
    target = jnp.sum((row_end[:, None, :] <= order[:, :, None]).astype(jnp.int32), axis=2)
    rank = order - jnp.take_along_axis(row_start, target, axis=1)
    arrival = jnp.take_along_axis(col_start, target, axis=1) + rank
    dst_keys = jax.random.split(jax.random.fold_in(key, 13), ndev)
    seats = jax.vmap(lambda kk: jax.random.permutation(kk, MEM_DEV))(dst_keys).astype(jnp.int32)
    slots = seats[target, arrival]
    return (target.reshape(-1).astype(jnp.int32), slots.reshape(-1).astype(jnp.int32))


def draw_dest(key, part):
    return route_plan(key)[0]


def draw_slot(key, part):
    return route_plan(key)[1]


def block_levels(rng, extent, cuts, least, largest):
    level = 1.0
    for axis_at, shards_of in cuts:
        steps = jax.random.uniform(jax.random.fold_in(jax.random.fold_in(rng, 6), axis_at), (shards_of,), jnp.float32, least / len(cuts), largest / len(cuts))
        level = level * jnp.repeat(jnp.exp(steps), extent[axis_at] // shards_of).reshape((-1,) + (1,) * (len(extent) - 1 - axis_at))
    return level


def scatter_about(own_key, extent, spread, reach, pieces=(), held_as=jnp.bfloat16):
    loudness = block_levels(own_key, extent, pieces, -0.22, 0.18) if pieces else 1.0
    entries = jax.random.normal(own_key, extent, jnp.float32) * spread * loudness
    return jnp.minimum(jnp.maximum(entries, -reach), reach).astype(held_as)


def setup_inputs(seed: int = 0) -> dict:
    keys = jax.random.split(jax.random.key(seed), 4)
    embed = scatter_about(keys[0], (DOCS, D), 1.0, 6.0, ((0, 128),))
    dest = draw_dest(jax.random.fold_in(keys[3], 71), 0)
    slot = draw_slot(jax.random.fold_in(keys[3], 71), 0)
    return {"embed": embed, "dest": dest, "slot": slot}


def reference(embed, dest, slot):
    position = dest * MEM_DEV + slot
    members = jnp.zeros((DOCS, D), jnp.bfloat16).at[position].set(embed)
    wide = members.astype(jnp.float32)
    unit = (wide * lax.rsqrt(lax.optimization_barrier(jnp.sum(wide * wide, axis=1, keepdims=True)) + 1e-06)).astype(jnp.bfloat16)
    groups = unit.reshape(N_GRP, CLUSTER, D)

    def per_group(group_unit):
        blocks = group_unit.reshape(N_BLK, MEM_DEV, D)

        def per_block(inputs):
            block, index = inputs
            scores = lax.dot_general(block, group_unit, (((1,), (1,)), ((), ())), preferred_element_type=jnp.float32)
            rows = index * MEM_DEV + jnp.arange(MEM_DEV, dtype=jnp.int32)
            cols = jnp.arange(CLUSTER, dtype=jnp.int32)
            scores = jnp.where(rows[:, None] == cols[None, :], jnp.float32(-3.0), scores)
            return lax.optimization_barrier(jnp.max(scores, axis=1))
        return lax.map(per_block, (blocks, jnp.arange(N_BLK, dtype=jnp.int32))).reshape(-1)
    best_member = lax.map(per_group, groups).reshape(-1)
    return best_member[position]
```

```python
import jax
import jax.numpy as jnp
from jax import lax
from jax.experimental import pallas as pl
from jax.experimental.pallas import tpu as pltpu
from jax.sharding import PartitionSpec as P

MESH = pl.DeviceIdType.MESH
GROUP = 64
N_MSG = 16
ROWS = GROUP * N_MSG
HALF = ROWS // 2
MARK = 4.0
LOW = -8.0

ORDER = [
    (0, 0, 0), (0, 2, 1), (1, 2, 1), (0, 1, 1), (1, 3, 1), (0, 3, 1), (1, 1, 1), (0, 2, 0),
    (1, 2, 0), (0, 1, 0), (1, 3, 0), (0, 3, 0), (1, 1, 0), (0, 0, 1), (1, 0, 1), (1, 0, 0),
]


def slot_of(s, d, f):
    return (d * 2 + f) * 2 + s


def place():
    g = lax.axis_index("grp")
    b = lax.axis_index("blk")
    x = (b // 4) * 2 + g // 8
    y = (g // 2) % 4
    z = b % 4
    c = g % 2
    return x, y, z, c


def device(x, y, z, c):
    return ((x % 2) * 8 + y * 2 + c, (x // 2) * 4 + z)


def flip(y, kind):
    low = y % 2
    return jnp.where(kind == 0, 3 - y, y + 1 - 2 * low)


def mate(y, kind):
    return flip(y, 1 - kind)


def routed(x, y, z, c, s, d, f, sign):
    here = c if s == 0 else 1 - c
    kind = here if sign == 1 else c
    step = (4 + sign * d) % 4
    yy = flip(y, kind) if f else y
    xx = jnp.where(kind == 0, lax.rem(x + step, 4), x)
    zz = jnp.where(kind == 0, z, lax.rem(z + step, 4))
    return device(xx, yy, zz, here)


def ring(x, y, z, c, step, paired):
    yy = mate(y, c) if paired else y
    xx = jnp.where(c == 0, x, lax.rem(x + step, 4))
    zz = jnp.where(c == 0, lax.rem(z + step, 4), z)
    return device(xx, yy, zz, c)


def nt(a, b):
    return lax.dot_general(a, b, (((1,), (1,)), ((), ())), preferred_element_type=jnp.float32)


def kernel(
    embed_ref, dest_ref, out_ref,
    unit, pack, blk_b, blk_a, blk_c, blk_e, low_b, low_a, low_c, low_e,
    max_b, max_a, max_c, max_e, got, table,
    pack_send, pack_recv, up_send, up_recv, down_send, down_recv, pair_send, pair_recv,
    part_send, part_recv, reply_send, reply_recv, self_sem,
):
    x, y, z, c = place()
    r = jnp.where(c == 0, z, x)
    wrapped = jnp.where(r >= 2, 1, 0)
    odd = y % 2

    barrier = pltpu.get_barrier_semaphore()
    partners = []
    for s, d, f in ORDER[1:]:
        partners.append(routed(x, y, z, c, s, d, f, -1))
    for s, d, f in ORDER[1:]:
        if s == 1 and (d, f) != (0, 0):
            partners.append(routed(x, y, z, c, s, d, f, 1))
    up = ring(x, y, z, c, 1, False)
    down = ring(x, y, z, c, 3, False)
    across = ring(x, y, z, c, 0, True)
    up_across = ring(x, y, z, c, 1, True)
    down_across = ring(x, y, z, c, 3, True)
    partners += [up, down, across, down_across]
    for other in partners:
        pl.semaphore_signal(barrier, inc=1, device_id=other, device_id_type=MESH)

    wide = embed_ref[...].astype(jnp.float32)
    scale = lax.rsqrt(jnp.sum(wide * wide, axis=1, keepdims=True) + 1e-06)
    unit[...] = (wide * scale).astype(jnp.bfloat16)

    dest = dest_ref[...]
    count = dest.shape[1]
    cluster = dest // 8
    kind = cluster // 8
    ring_at = (cluster // 2) % 4
    pair_at = cluster % 2
    s_of = jnp.where(kind == c, 0, 1)
    d_of = jnp.where(kind == 0, ring_at + 4 - x, ring_at + 4 - z) % 4
    my_pair0 = y // 2
    my_pair1 = ((y + 1) % 4) // 2
    f_of = jnp.where(jnp.where(kind == 0, my_pair0, my_pair1) == pair_at, 0, 1)
    code = (d_of * 2 + f_of) * 2 + s_of
    message = jnp.zeros_like(code)
    for j, (s, d, f) in enumerate(ORDER):
        message = jnp.where(code == slot_of(s, d, f), j, message)
    mine = lax.broadcasted_iota(jnp.int32, (N_MSG, count), 0) == message
    earlier = (
        lax.broadcasted_iota(jnp.int32, (count, count), 0)
        < lax.broadcasted_iota(jnp.int32, (count, count), 1)
    ).astype(jnp.float32).astype(jnp.bfloat16)
    mine_f = mine.astype(jnp.float32)
    before = jnp.dot(mine_f.astype(jnp.bfloat16), earlier, preferred_element_type=jnp.float32)
    rank = jnp.sum(before * mine_f, axis=0, keepdims=True).astype(jnp.int32)
    position = message * GROUP + rank

    def send(j):
        s, d, f = ORDER[j]
        rows = pl.ds(slot_of(s, d, f) * GROUP, GROUP)
        return pltpu.make_async_remote_copy(
            src_ref=pack.at[pl.ds(j * GROUP, GROUP)], dst_ref=blk_b.at[rows],
            send_sem=pack_send.at[j], recv_sem=pack_recv.at[j],
            device_id=routed(x, y, z, c, s, d, f, 1), device_id_type=MESH,
        )

    def spread(j, upward):
        rows = pl.ds(slot_of(*ORDER[j]) * GROUP, GROUP)
        return pltpu.make_async_remote_copy(
            src_ref=blk_b.at[rows], dst_ref=(blk_a if upward else blk_c).at[rows],
            send_sem=(up_send if upward else down_send).at[j],
            recv_sem=(up_recv if upward else down_recv).at[j],
            device_id=up if upward else down, device_id_type=MESH,
        )

    def relay(j):
        rows = pl.ds(slot_of(*ORDER[j]) * GROUP, GROUP)
        return pltpu.make_async_remote_copy(
            src_ref=blk_c.at[rows], dst_ref=blk_e.at[rows],
            send_sem=pair_send.at[j], recv_sem=pair_recv.at[j],
            device_id=across, device_id_type=MESH,
        )

    part = 4
    size = ROWS // part
    for k in range(part):
        at = lax.broadcasted_iota(jnp.int32, (size, count), 0) + k * size
        pick = (at == position).astype(jnp.float32)
        rows = jnp.dot(pick.astype(jnp.bfloat16), unit[...], preferred_element_type=jnp.float32)
        empty = jnp.sum(pick, axis=1, keepdims=True) < 0.5
        lane = lax.broadcasted_iota(jnp.int32, (size, 128), 1)
        first = jnp.where(empty & (lane == 0), MARK, rows[:, :128])
        packed = jnp.concatenate([first, rows[:, 128:]], axis=1).astype(jnp.bfloat16)
        if k == 0:
            blk_b[pl.ds(0, GROUP), :] = packed[:GROUP]
            pack[pl.ds(GROUP, size - GROUP), :] = packed[GROUP:]
            pl.semaphore_wait(barrier, len(partners))
        else:
            pack[pl.ds(k * size, size), :] = packed
        for j in range(k * size // GROUP, (k + 1) * size // GROUP):
            if j == 0:
                spread(0, True).start()
                spread(0, False).start()
            else:
                send(j).start()

    for j in range(1, N_MSG):
        send(j).wait_recv()
        spread(j, True).start()
        spread(j, False).start()

    ones = jnp.where(lax.broadcasted_iota(jnp.int32, (16, 128), 1) == 0, 1.0, 0.0).astype(jnp.bfloat16)

    def lows(block, low):
        marks = nt(ones, block[:, :128])[0:1]
        low[...] = jnp.where(marks > 2.0, LOW, 0.0)

    def product(left, l0, left_max, right, r0, right_low, right_max, same=False):
        scores = nt(left[pl.ds(l0, HALF), :], right[pl.ds(r0, HALF), :])
        if same:
            at0 = lax.broadcasted_iota(jnp.int32, (HALF, HALF), 0)
            at1 = lax.broadcasted_iota(jnp.int32, (HALF, HALF), 1)
            scores = jnp.where(at0 == at1, LOW, scores)
        marks = left[pl.ds(l0, HALF), 0:1].astype(jnp.float32)
        scores = scores + jnp.where(marks > 2.0, LOW, 0.0)
        down_max = jnp.max(scores, axis=0, keepdims=True)
        q0 = r0 // 128
        for q in range(HALF // 128):
            right_max[q0 + q] = jnp.maximum(right_max[q0 + q], down_max[:, q * 128 : (q + 1) * 128])
        if left_max is not None:
            wide = scores + right_low[...][:, r0 : r0 + HALF] if isinstance(r0, int) else scores + low_half(right_low, r0)
            best = jnp.maximum(
                jnp.maximum(wide[:, 0:128], wide[:, 128:256]), jnp.maximum(wide[:, 256:384], wide[:, 384:512])
            )
            for q in range(HALF // 128):
                turned = best[q * 128 : (q + 1) * 128, :].T
                left_max[l0 // 128 + q] = jnp.maximum(
                    left_max[l0 // 128 + q], jnp.max(turned, axis=0, keepdims=True)
                )

    def low_half(low, r0):
        return jnp.where(r0 == 0, low[...][:, :HALF], low[...][:, HALF:])

    for ref in (max_b, max_a, max_c, max_e):
        ref[...] = jnp.full(ref.shape, LOW, jnp.float32)

    lows(blk_b, low_b)
    product(blk_b, 0, None, blk_b, 0, low_b, max_b, same=True)
    product(blk_b, HALF, None, blk_b, HALF, low_b, max_b, same=True)
    product(blk_b, 0, max_b, blk_b, HALF, low_b, max_b)

    for j in range(N_MSG):
        spread(j, False).wait_recv()
        relay(j).start()
    lows(blk_c, low_c)
    for l0 in (0, HALF):
        for r0 in (0, HALF):
            product(blk_b, l0, max_b, blk_c, r0, low_c, max_c)
    for j in range(N_MSG):
        spread(j, True).wait_recv()
    for k in range(2):
        product(blk_a, k * HALF, max_a, blk_c, (wrapped + k) % 2 * HALF, low_c, max_c)
    for j in range(N_MSG):
        relay(j).wait_recv()
    lows(blk_e, low_e)
    for l0 in (0, HALF):
        for r0 in (0, HALF):
            product(blk_b, l0, max_b, blk_e, r0, low_e, max_e)
    for k in range(2):
        product(blk_a, k * HALF, max_a, blk_e, (wrapped + k) % 2 * HALF, low_e, max_e)
        product(blk_c, k * HALF, max_c, blk_e, (odd + k) % 2 * HALF, low_e, max_e)

    parts = [
        pltpu.make_async_remote_copy(
            src_ref=ref, dst_ref=got.at[n], send_sem=part_send.at[n], recv_sem=part_recv.at[n],
            device_id=other, device_id_type=MESH,
        )
        for n, (ref, other) in enumerate(((max_a, down), (max_c, up), (max_e, up_across)))
    ]
    for copy in parts:
        copy.start()
    for copy in parts:
        copy.wait_recv()
    max_b[...] = jnp.maximum(jnp.maximum(max_b[...], got[0]), jnp.maximum(got[1], got[2]))

    replies = []
    for j, (s, d, f) in enumerate(ORDER):
        if j == 0:
            continue
        replies.append(
            pltpu.make_async_remote_copy(
                src_ref=max_b.at[d * 2 + f], dst_ref=table.at[j],
                send_sem=reply_send.at[j], recv_sem=reply_recv.at[j],
                device_id=routed(x, y, z, c, s, d, f, -1), device_id_type=MESH,
            )
        )
    for copy in replies:
        copy.start()
    table[0] = max_b[0]
    for copy in replies:
        copy.wait_recv()

    values = jnp.concatenate([table[j] for j in range(N_MSG)], axis=0)
    high = values.astype(jnp.bfloat16)
    rest = values - high.astype(jnp.float32)
    mid = rest.astype(jnp.bfloat16)
    last = (rest - mid.astype(jnp.float32)).astype(jnp.bfloat16)
    choose = mine_f.astype(jnp.bfloat16)

    def taken(v):
        return lax.dot_general(v, choose, (((0,), (0,)), ((), ())), preferred_element_type=jnp.float32)

    lanes = taken(high) + taken(mid) + taken(last)
    want = s_of * GROUP + rank
    at = lax.broadcasted_iota(jnp.int32, (128, count), 0)
    out_ref[...] = jnp.sum(jnp.where(at == want, lanes, 0.0), axis=0, keepdims=True)

    for j in range(N_MSG):
        if j:
            send(j).wait_send()
        spread(j, True).wait_send()
        spread(j, False).wait_send()
        relay(j).wait_send()
    for copy in parts + replies:
        copy.wait_send()


def on_device(embed, dest, slot):
    count = embed.shape[0]
    width = embed.shape[1]
    vmem = pl.BlockSpec(memory_space=pltpu.VMEM)
    block = pltpu.VMEM((ROWS, width), jnp.bfloat16)
    low = pltpu.VMEM((1, ROWS), jnp.float32)
    best = pltpu.VMEM((ROWS // 128, 1, 128), jnp.float32)
    dma = pltpu.SemaphoreType.DMA
    out = pl.pallas_call(
        kernel,
        out_shape=jax.ShapeDtypeStruct((1, count), jnp.float32),
        in_specs=[vmem, vmem],
        out_specs=vmem,
        scratch_shapes=[
            pltpu.VMEM((count, width), jnp.bfloat16), block, block, block, block, block, low, low, low, low,
            best, best, best, best,
            pltpu.VMEM((3, ROWS // 128, 1, 128), jnp.float32), pltpu.VMEM((N_MSG, 1, 128), jnp.float32),
        ]
        + [dma((N_MSG,))] * 8
        + [dma((3,)), dma((3,)), dma((N_MSG,)), dma((N_MSG,)), dma(())],
        compiler_params=pltpu.CompilerParams(
            collective_id=0, has_side_effects=True, vmem_limit_bytes=48 * 2**20
        ),
        cost_estimate=pl.CostEstimate(flops=11 * 10**9, bytes_accessed=2 * 2**20, transcendentals=512),
    )(embed, dest.reshape(1, count))
    return out.reshape(count)


def solution(mesh):
    placed = (P(("grp", "blk"), None), P(("grp", "blk")), P(("grp", "blk")))
    return jax.shard_map(
        on_device, mesh=mesh, in_specs=placed, out_specs=P(("grp", "blk")), check_vma=False
    )
```

```python
import jax
import jax.numpy as jnp
from jax import lax
from jax.experimental import pallas as pl
from jax.experimental.pallas import tpu as pltpu
from jax.sharding import PartitionSpec as P

MESH = pl.DeviceIdType.MESH
LAG = 4
GROUP = 64
N_MSG = 16
ROWS = GROUP * N_MSG
PIECE = 256
MARK = 4.0
LOW = -8.0

ORDER = [
    (0, 0, 0), (1, 0, 0), (0, 1, 0), (1, 1, 0), (0, 3, 0), (1, 3, 0), (0, 0, 1), (1, 0, 1),
    (0, 2, 0), (1, 2, 0), (0, 1, 1), (1, 1, 1), (0, 3, 1), (1, 3, 1), (0, 2, 1), (1, 2, 1),
]


def place():
    g = lax.axis_index("grp")
    b = lax.axis_index("blk")
    x = ((b >> 2) << 1) + (g >> 3)
    return x, (g >> 1) & 3, b & 3, g & 1


def device(x, y, z, c):
    return (((x & 1) << 3) + (y << 1) + c, ((x >> 1) << 2) + z)


def flip(y, kind):
    return jnp.where(kind == 0, 3 - y, y + 1 - 2 * (y & 1))


def mate(y, kind):
    return flip(y, 1 - kind)


def routed(x, y, z, c, s, d, f, sign):
    here = c if s == 0 else 1 - c
    kind = here if sign == 1 else c
    step = sign * d
    yy = flip(y, kind) if f else y
    xx = jnp.where(kind == 0, (x + step) & 3, x)
    zz = jnp.where(kind == 0, z, (z + step) & 3)
    return device(xx, yy, zz, here)


def ring(x, y, z, c, step, paired):
    yy = mate(y, c) if paired else y
    xx = jnp.where(c == 0, x, (x + step) & 3)
    zz = jnp.where(c == 0, (z + step) & 3, z)
    return device(xx, yy, zz, c)


def nt(a, b):
    return lax.dot_general(a, b, (((1,), (1,)), ((), ())), preferred_element_type=jnp.float32)


def kernel(
    embed_hbm, dest_hbm, out_ref,
    embed_ref, dest_ref, load_sem, unit, pack, blk_b, blk_a, blk_c, blk_e, low_b, low_a, low_c, low_e,
    max_b, max_a, max_c, max_e, got, table,
    pack_send, pack_recv, up_send, up_recv, down_send, down_recv, pair_send, pair_recv,
    part_send, part_recv, reply_send, reply_recv,
):
    x, y, z, c = place()
    embed_in = pltpu.make_async_copy(embed_hbm, embed_ref, load_sem.at[0])
    dest_in = pltpu.make_async_copy(dest_hbm, dest_ref, load_sem.at[1])
    dest_in.start()
    embed_in.start()

    barrier = pltpu.get_barrier_semaphore()
    partners = []
    for s, d, f in ORDER[1:]:
        partners.append(routed(x, y, z, c, s, d, f, -1))
    for s, d, f in ORDER[1:]:
        if s == 1 and (d, f) != (0, 0):
            partners.append(routed(x, y, z, c, s, d, f, 1))
    up = ring(x, y, z, c, 1, False)
    down = ring(x, y, z, c, 3, False)
    across = ring(x, y, z, c, 0, True)
    up_across = ring(x, y, z, c, 1, True)
    down_across = ring(x, y, z, c, 3, True)
    partners += [up, down, across, down_across]
    for other in partners:
        pl.semaphore_signal(barrier, inc=1, device_id=other, device_id_type=MESH)

    dest_in.wait()
    dest = dest_ref[...]
    count = dest.shape[1]
    cluster = dest >> 3
    kind = cluster >> 3
    ring_at = (cluster >> 1) & 3
    pair_at = cluster & 1
    s_of = jnp.where(kind == c, 0, 1)
    d_of = (jnp.where(kind == 0, ring_at - x, ring_at - z)) & 3
    my_pair0 = y >> 1
    my_pair1 = ((y + 1) & 3) >> 1
    f_of = jnp.where(jnp.where(kind == 0, my_pair0, my_pair1) == pair_at, 0, 1)
    code = (d_of * 2 + f_of) * 2 + s_of
    message = jnp.zeros_like(code)
    for j, (s, d, f) in enumerate(ORDER):
        message = jnp.where(code == (d * 2 + f) * 2 + s, j, message)
    mine = lax.broadcasted_iota(jnp.int32, (N_MSG, count), 0) == message
    earlier = (
        lax.broadcasted_iota(jnp.int32, (count, count), 0)
        < lax.broadcasted_iota(jnp.int32, (count, count), 1)
    ).astype(jnp.float32).astype(jnp.bfloat16)
    mine_f = mine.astype(jnp.float32)
    before = jnp.dot(mine_f.astype(jnp.bfloat16), earlier, preferred_element_type=jnp.float32)
    rank = jnp.sum(before * mine_f, axis=0, keepdims=True).astype(jnp.int32)
    position = message * GROUP + rank

    embed_in.wait()
    wide = embed_ref[...].astype(jnp.float32)
    scale = lax.rsqrt(jnp.sum(wide * wide, axis=1, keepdims=True) + 1e-06)
    unit[...] = (wide * scale).astype(jnp.bfloat16)


    def send(j):
        s, d, f = ORDER[j]
        rows = pl.ds(j * GROUP, GROUP)
        return pltpu.make_async_remote_copy(
            src_ref=pack.at[pl.ds(j * GROUP, GROUP)], dst_ref=blk_b.at[rows],
            send_sem=pack_send.at[j], recv_sem=pack_recv.at[j],
            device_id=routed(x, y, z, c, s, d, f, 1), device_id_type=MESH,
        )

    def spread(j, upward):
        rows = pl.ds(j * GROUP, GROUP)
        return pltpu.make_async_remote_copy(
            src_ref=blk_b.at[rows], dst_ref=(blk_a if upward else blk_c).at[rows],
            send_sem=(up_send if upward else down_send).at[j],
            recv_sem=(up_recv if upward else down_recv).at[j],
            device_id=up if upward else down, device_id_type=MESH,
        )

    def relay(j):
        rows = pl.ds(j * GROUP, GROUP)
        return pltpu.make_async_remote_copy(
            src_ref=blk_c.at[rows], dst_ref=blk_e.at[rows],
            send_sem=pair_send.at[j], recv_sem=pair_recv.at[j],
            device_id=across, device_id_type=MESH,
        )

    part = 4
    size = ROWS // part
    for k in range(part):
        at = lax.broadcasted_iota(jnp.int32, (size, count), 0) + k * size
        pick = (at == position).astype(jnp.float32)
        rows = jnp.dot(pick.astype(jnp.bfloat16), unit[...], preferred_element_type=jnp.float32)
        empty = jnp.sum(pick, axis=1, keepdims=True) < 0.5
        lane = lax.broadcasted_iota(jnp.int32, (size, 128), 1)
        first = jnp.where(empty & (lane == 0), MARK, rows[:, :128])
        packed = jnp.concatenate([first, rows[:, 128:]], axis=1).astype(jnp.bfloat16)
        if k == 0:
            blk_b[pl.ds(0, GROUP), :] = packed[:GROUP]
            pack[pl.ds(GROUP, size - GROUP), :] = packed[GROUP:]
            pl.semaphore_wait(barrier, len(partners))
        else:
            pack[pl.ds(k * size, size), :] = packed
        for j in range(k * size // GROUP, (k + 1) * size // GROUP):
            if j == 0:
                spread(0, True).start()
                spread(0, False).start()
            else:
                send(j).start()

    ones = jnp.where(lax.broadcasted_iota(jnp.int32, (16, 128), 1) == 0, 1.0, 0.0).astype(jnp.bfloat16)
    blocks = {"a": (blk_a, low_a, max_a), "b": (blk_b, low_b, max_b), "c": (blk_c, low_c, max_c), "e": (blk_e, low_e, max_e)}
    here = {name: [] for name in blocks}

    def meets(one, i, two, j):
        if one == two:
            return one == "b"
        if "b" in (one, two):
            return "a" not in (one, two)
        if one == "e" or (one == "a" and two == "c"):
            i, j = j, i
        return i >= j

    def compare(name, q):
        block, low, left_max = blocks[name]
        rows = block[pl.ds(q * PIECE, PIECE), :]
        marks = nt(ones, rows[:, :128])[0:1]
        low[:, pl.ds(q * PIECE, PIECE)] = jnp.where(marks > 2.0, LOW, 0.0)
        here[name].append(q)
        spans = []
        for other in blocks:
            run = None
            for k in range(ROWS // PIECE + 1):
                if k in here[other] and meets(name, q, other, k):
                    run = k if run is None else run
                elif run is not None:
                    spans.append((other, run * PIECE, (k - run) * PIECE))
                    run = None
        if not spans:
            return
        tilt = jnp.where(rows[:, 0:1].astype(jnp.float32) > 2.0, LOW, 0.0)
        best = None
        for other, start, width in spans:
            right, right_low, right_max = blocks[other]
            scores = nt(rows, right[pl.ds(start, width), :]) + tilt
            if other == name:
                at0 = lax.broadcasted_iota(jnp.int32, scores.shape, 0) + q * PIECE
                at1 = lax.broadcasted_iota(jnp.int32, scores.shape, 1) + start
                scores = jnp.where(at0 == at1, LOW, scores)
            tops = jnp.max(scores, axis=0, keepdims=True)
            for n in range(width // 128):
                at = start // 128 + n
                right_max[at] = jnp.maximum(right_max[at], tops[:, n * 128 : (n + 1) * 128])
            scores = scores + right_low[:, pl.ds(start, width)]
            for n in range(width // 128):
                tile = scores[:, n * 128 : (n + 1) * 128]
                best = tile if best is None else jnp.maximum(best, tile)
        for n in range(PIECE // 128):
            turned = best[n * 128 : (n + 1) * 128, :].T
            at = q * (PIECE // 128) + n
            left_max[at] = jnp.maximum(left_max[at], jnp.max(turned, axis=0, keepdims=True))

    per = PIECE // GROUP
    last = ROWS // PIECE - 1

    def of_piece(q):
        return range(q * per, (q + 1) * per)

    def compare_e(q):
        for j in of_piece(q):
            relay(j).wait_recv()
        compare("e", q)

    def passed(j):
        spread(j, False).wait_recv()
        relay(j).start()
        if j % per == per - 1:
            q = j // per
            compare("c", q)
            for k in of_piece(q):
                spread(k, True).wait_recv()
            compare("a", q)
        if j % per == 1 and j > per:
            compare_e(j // per - 1)

    for ref in (max_b, max_a, max_c, max_e):
        ref[...] = jnp.full(ref.shape, LOW, jnp.float32)
    for j in range(N_MSG):
        if j:
            send(j).wait_recv()
            spread(j, True).start()
            spread(j, False).start()
        if j >= LAG:
            passed(j - LAG)
        if j % per == per - 1:
            compare("b", j // per)
    for j in range(N_MSG - LAG, N_MSG):
        passed(j)
    compare_e(last)

    parts = [
        pltpu.make_async_remote_copy(
            src_ref=ref, dst_ref=got.at[n], send_sem=part_send.at[n], recv_sem=part_recv.at[n],
            device_id=other, device_id_type=MESH,
        )
        for n, (ref, other) in enumerate(((max_a, down), (max_c, up), (max_e, up_across)))
    ]
    for copy in parts:
        copy.start()
    for copy in parts:
        copy.wait_recv()
    max_b[...] = jnp.maximum(jnp.maximum(max_b[...], got[0]), jnp.maximum(got[1], got[2]))

    replies = []
    for j, (s, d, f) in enumerate(ORDER):
        if j == 0:
            continue
        replies.append(
            pltpu.make_async_remote_copy(
                src_ref=max_b.at[j // 2], dst_ref=table.at[j],
                send_sem=reply_send.at[j], recv_sem=reply_recv.at[j],
                device_id=routed(x, y, z, c, s, d, f, -1), device_id_type=MESH,
            )
        )
    for copy in replies:
        copy.start()
    table[0] = max_b[0]
    for copy in replies:
        copy.wait_recv()

    values = jnp.concatenate([table[j] for j in range(N_MSG)], axis=0)
    high = values.astype(jnp.bfloat16)
    rest = values - high.astype(jnp.float32)
    mid = rest.astype(jnp.bfloat16)
    last = (rest - mid.astype(jnp.float32)).astype(jnp.bfloat16)
    choose = mine_f.astype(jnp.bfloat16)

    def taken(v):
        return lax.dot_general(v, choose, (((0,), (0,)), ((), ())), preferred_element_type=jnp.float32)

    lanes = taken(high) + taken(mid) + taken(last)
    want = (message & 1) * GROUP + rank
    at = lax.broadcasted_iota(jnp.int32, (128, count), 0)
    out_ref[...] = jnp.sum(jnp.where(at == want, lanes, 0.0), axis=0, keepdims=True)

    for j in range(N_MSG):
        if j:
            send(j).wait_send()
        spread(j, True).wait_send()
        spread(j, False).wait_send()
        relay(j).wait_send()
    for copy in parts + replies:
        copy.wait_send()


def on_device(embed, dest, slot):
    count = embed.shape[0]
    width = embed.shape[1]
    vmem = pl.BlockSpec(memory_space=pltpu.VMEM)
    block = pltpu.VMEM((ROWS, width), jnp.bfloat16)
    low = pltpu.VMEM((1, ROWS), jnp.float32)
    best = pltpu.VMEM((ROWS // 128, 1, 128), jnp.float32)
    dma = pltpu.SemaphoreType.DMA
    out = pl.pallas_call(
        kernel,
        out_shape=jax.ShapeDtypeStruct((1, count), jnp.float32),
        in_specs=[pl.BlockSpec(memory_space=pl.ANY)] * 2,
        out_specs=vmem,
        scratch_shapes=[
            pltpu.VMEM((count, width), jnp.bfloat16), pltpu.VMEM((1, count), jnp.int32), dma((2,)),
            pltpu.VMEM((count, width), jnp.bfloat16), block, block, block, block, block, low, low, low, low,
            best, best, best, best,
            pltpu.VMEM((3, ROWS // 128, 1, 128), jnp.float32), pltpu.VMEM((N_MSG, 1, 128), jnp.float32),
        ]
        + [dma((N_MSG,))] * 8
        + [dma((3,)), dma((3,)), dma((N_MSG,)), dma((N_MSG,))],
        compiler_params=pltpu.CompilerParams(
            collective_id=0, has_side_effects=True, vmem_limit_bytes=60 * 2**20
        ),
        cost_estimate=pl.CostEstimate(flops=11 * 10**9, bytes_accessed=2 * 2**20, transcendentals=512),
    )(embed, dest.reshape(1, count))
    return out.reshape(count)


def solution(mesh):
    placed = (P(("grp", "blk"), None), P(("grp", "blk")), P(("grp", "blk")))
    return jax.shard_map(
        on_device, mesh=mesh, in_specs=placed, out_specs=P(("grp", "blk")), check_vma=False
    )
```

```python
import functools

import jax
import jax.numpy as jnp
from jax import lax
from jax.experimental import pallas as pl
from jax.experimental.pallas import tpu as pltpu
from jax.sharding import PartitionSpec as P

MESH = pl.DeviceIdType.MESH
BUDGET = 1024
LATER = 2
LAG = 4
GROUP = 64
N_MSG = 16
ROWS = GROUP * N_MSG
PIECE = 256
MARK = 4.0
LOW = -8.0

ORDER = [
    (0, 0, 0), (1, 0, 0), (0, 1, 0), (1, 1, 0), (0, 3, 0), (1, 3, 0), (0, 0, 1), (1, 0, 1),
    (0, 2, 0), (1, 2, 0), (0, 1, 1), (1, 1, 1), (0, 3, 1), (1, 3, 1), (0, 2, 1), (1, 2, 1),
]


PER = PIECE // GROUP
LATE = ORDER[N_MSG - PER :]


def place():
    g = lax.axis_index("grp")
    b = lax.axis_index("blk")
    x = ((b >> 2) << 1) + (g >> 3)
    return x, (g >> 1) & 3, b & 3, g & 1


def device(x, y, z, c):
    return (((x & 1) << 3) + (y << 1) + c, ((x >> 1) << 2) + z)


def flip(y, kind):
    return jnp.where(kind == 0, 3 - y, y + 1 - 2 * (y & 1))


def mate(y, kind):
    return flip(y, 1 - kind)


def routed(x, y, z, c, s, d, f, sign):
    return device(*end_of(x, y, z, c, s, d, f, sign))


def end_of(x, y, z, c, s, d, f, sign):
    here = c if s == 0 else 1 - c
    kind = here if sign == 1 else c
    step = sign * d
    yy = flip(y, kind) if f else y
    xx = jnp.where(kind == 0, (x + step) & 3, x)
    zz = jnp.where(kind == 0, z, (z + step) & 3)
    return xx, yy, zz, here


def moved(x, y, z, c, step, paired):
    yy = mate(y, c) if paired else y
    xx = jnp.where(c == 0, x, (x + step) & 3)
    zz = jnp.where(c == 0, (z + step) & 3, z)
    return xx, yy, zz, c


def ring(x, y, z, c, step, paired):
    return device(*moved(x, y, z, c, step, paired))


def nt(a, b):
    return lax.dot_general(a, b, (((1,), (1,)), ((), ())), preferred_element_type=jnp.float32)


def kernel(
    embed_hbm, dest_hbm, out_ref,
    embed_ref, dest_ref, load_sem, unit, pack, blk_b, blk_a, blk_c, blk_e, low_b, low_a, low_c, low_e,
    max_b, max_a, max_c, max_e, got, table, extra,
    pack_send, pack_recv, up_send, up_recv, down_send, down_recv, pair_send, pair_recv,
    part_send, part_recv, reply_send, reply_recv, answer_send, answer_recv,
):
    x, y, z, c = place()
    embed_in = pltpu.make_async_copy(embed_hbm, embed_ref, load_sem.at[0])
    dest_in = pltpu.make_async_copy(dest_hbm, dest_ref, load_sem.at[1])
    dest_in.start()
    embed_in.start()

    barrier = pltpu.get_barrier_semaphore()
    partners = []
    for s, d, f in ORDER[1:]:
        partners.append(routed(x, y, z, c, s, d, f, -1))
    for s, d, f in ORDER[1:]:
        if s == 1 and (d, f) != (0, 0):
            partners.append(routed(x, y, z, c, s, d, f, 1))
    up = ring(x, y, z, c, 1, False)
    down = ring(x, y, z, c, 3, False)
    across = ring(x, y, z, c, 0, True)
    up_across = ring(x, y, z, c, 1, True)
    down_across = ring(x, y, z, c, 3, True)
    partners += [up, down, across, down_across]
    for s, d, f in LATE:
        partners.append(ring(*end_of(x, y, z, c, s, d, f, 1), 3, True))
    for other in partners:
        pl.semaphore_signal(barrier, inc=1, device_id=other, device_id_type=MESH)

    dest_in.wait()
    dest = dest_ref[...]
    count = dest.shape[1]
    cluster = dest >> 3
    kind = cluster >> 3
    ring_at = (cluster >> 1) & 3
    pair_at = cluster & 1
    s_of = jnp.where(kind == c, 0, 1)
    d_of = (jnp.where(kind == 0, ring_at - x, ring_at - z)) & 3
    my_pair0 = y >> 1
    my_pair1 = ((y + 1) & 3) >> 1
    f_of = jnp.where(jnp.where(kind == 0, my_pair0, my_pair1) == pair_at, 0, 1)
    code = (d_of * 2 + f_of) * 2 + s_of
    message = jnp.zeros_like(code)
    for j, (s, d, f) in enumerate(ORDER):
        message = jnp.where(code == (d * 2 + f) * 2 + s, j, message)
    mine = lax.broadcasted_iota(jnp.int32, (N_MSG, count), 0) == message
    earlier = (
        lax.broadcasted_iota(jnp.int32, (count, count), 0)
        < lax.broadcasted_iota(jnp.int32, (count, count), 1)
    ).astype(jnp.float32).astype(jnp.bfloat16)
    mine_f = mine.astype(jnp.float32)
    before = jnp.dot(mine_f.astype(jnp.bfloat16), earlier, preferred_element_type=jnp.float32)
    rank = jnp.sum(before * mine_f, axis=0, keepdims=True).astype(jnp.int32)
    position = message * GROUP + rank

    embed_in.wait()
    wide = embed_ref[...].astype(jnp.float32)
    scale = lax.rsqrt(jnp.sum(wide * wide, axis=1, keepdims=True) + 1e-06)
    unit[...] = (wide * scale).astype(jnp.bfloat16)


    def send(j):
        s, d, f = ORDER[j]
        rows = pl.ds(j * GROUP, GROUP)
        return pltpu.make_async_remote_copy(
            src_ref=pack.at[pl.ds(j * GROUP, GROUP)], dst_ref=blk_b.at[rows],
            send_sem=pack_send.at[j], recv_sem=pack_recv.at[j],
            device_id=routed(x, y, z, c, s, d, f, 1), device_id_type=MESH,
        )

    def spread(j, upward):
        rows = pl.ds(j * GROUP, GROUP)
        return pltpu.make_async_remote_copy(
            src_ref=blk_b.at[rows], dst_ref=(blk_a if upward else blk_c).at[rows],
            send_sem=(up_send if upward else down_send).at[j],
            recv_sem=(up_recv if upward else down_recv).at[j],
            device_id=up if upward else down, device_id_type=MESH,
        )

    def relay(j):
        rows = pl.ds(j * GROUP, GROUP)
        return pltpu.make_async_remote_copy(
            src_ref=blk_c.at[rows], dst_ref=blk_e.at[rows],
            send_sem=pair_send.at[j], recv_sem=pair_recv.at[j],
            device_id=across, device_id_type=MESH,
        )

    part = 4
    size = ROWS // part
    for k in range(part):
        at = lax.broadcasted_iota(jnp.int32, (size, count), 0) + k * size
        pick = (at == position).astype(jnp.float32)
        rows = jnp.dot(pick.astype(jnp.bfloat16), unit[...], preferred_element_type=jnp.float32)
        empty = jnp.sum(pick, axis=1, keepdims=True) < 0.5
        lane = lax.broadcasted_iota(jnp.int32, (size, 128), 1)
        first = jnp.where(empty & (lane == 0), MARK, rows[:, :128])
        packed = jnp.concatenate([first, rows[:, 128:]], axis=1).astype(jnp.bfloat16)
        if k == 0:
            blk_b[pl.ds(0, GROUP), :] = packed[:GROUP]
            pack[pl.ds(GROUP, size - GROUP), :] = packed[GROUP:]
            pl.semaphore_wait(barrier, len(partners))
        else:
            pack[pl.ds(k * size, size), :] = packed
        for j in range(k * size // GROUP, (k + 1) * size // GROUP):
            if j == 0:
                spread(0, True).start()
                spread(0, False).start()
            else:
                send(j).start()

    ones = jnp.where(lax.broadcasted_iota(jnp.int32, (16, 128), 1) == 0, 1.0, 0.0).astype(jnp.bfloat16)
    blocks = {"a": (blk_a, low_a, max_a), "c": (blk_c, low_c, max_c), "e": (blk_e, low_e, max_e), "b": (blk_b, low_b, max_b)}
    here = {name: [] for name in blocks}

    def meets(one, i, two, j):
        if one == two:
            return one == "b"
        if "b" in (one, two):
            return "a" not in (one, two)
        if one == "e" or (one == "a" and two == "c"):
            i, j = j, i
        return i >= j

    def compare(name, q):
        block, low, left_max = blocks[name]
        rows = block[pl.ds(q * PIECE, PIECE), :]
        marks = nt(ones, rows[:, :128])[0:1]
        low[:, pl.ds(q * PIECE, PIECE)] = jnp.where(marks > 2.0, LOW, 0.0)
        here[name].append(q)
        spans = []
        for other in blocks:
            run = None
            once = name == "e" and other in ("a", "c")
            if once:
                spans.append((other, q * PIECE, PIECE))
            for k in range(ROWS // PIECE + 1):
                if k in here[other] and meets(name, q, other, k) and not (once and k == q):
                    run = k if run is None else run
                elif run is not None:
                    spans.append((other, run * PIECE, (k - run) * PIECE))
                    run = None
        for other, start, width in spans:
            for at in range(start, start + width, 2 * PIECE):
                wide = min(2 * PIECE, start + width - at)
                waiting.append((wide, functools.partial(product, name, q, other, at, wide)))

    def product(name, q, other, start, width):
        block, low, left_max = blocks[name]
        right, right_low, right_max = blocks[other]
        rows = block[pl.ds(q * PIECE, PIECE), :]
        tilt = jnp.where(rows[:, 0:1].astype(jnp.float32) > 2.0, LOW, 0.0)
        scores = nt(rows, right[pl.ds(start, width), :]) + tilt
        if other == name:
            at0 = lax.broadcasted_iota(jnp.int32, scores.shape, 0) + q * PIECE
            at1 = lax.broadcasted_iota(jnp.int32, scores.shape, 1) + start
            scores = jnp.where(at0 == at1, LOW, scores)
        if not (name == "e" and other in ("a", "c") and start == q * PIECE):
            tops = jnp.max(scores, axis=0, keepdims=True)
            for n in range(width // 128):
                at = start // 128 + n
                right_max[at] = jnp.maximum(right_max[at], tops[:, n * 128 : (n + 1) * 128])
        scores = scores + right_low[:, pl.ds(start, width)]
        best = None
        for n in range(width // 128):
            tile = scores[:, n * 128 : (n + 1) * 128]
            best = tile if best is None else jnp.maximum(best, tile)
        for n in range(PIECE // 128):
            turned = best[n * 128 : (n + 1) * 128, :].T
            at = q * (PIECE // 128) + n
            left_max[at] = jnp.maximum(left_max[at], jnp.max(turned, axis=0, keepdims=True))

    def work(budget):
        while waiting and budget > 0:
            wide, step = waiting.pop(0)
            step()
            budget -= wide

    waiting = []
    last = ROWS // PIECE - 1

    def of_piece(q):
        return range(q * PER, (q + 1) * PER)

    def compare_e(q):
        for j in of_piece(q):
            relay(j).wait_recv()
        compare("e", q)

    for ref in (max_b, max_a, max_c, max_e):
        ref[...] = jnp.full(ref.shape, LOW, jnp.float32)
    for step in range(N_MSG + LAG):
        j, k = step, step - LAG
        if 0 < j < N_MSG:
            send(j).wait_recv()
            spread(j, True).start()
            spread(j, False).start()
        if k >= 0:
            spread(k, False).wait_recv()
            relay(k).start()
        if j < N_MSG and j % PER == PER - 1:
            compare("b", j // PER)
        if k >= 0 and k % PER == PER - 1:
            compare("c", k // PER)
            for n in of_piece(k // PER):
                spread(n, True).wait_recv()
            compare("a", k // PER)
        if k >= PER and (k - LATER) % PER == PER - 1 and (k - LATER) // PER < last:
            compare_e((k - LATER) // PER)
        if step < N_MSG + LAG - 1:
            work(BUDGET)
    work(ROWS * ROWS)

    early = pl.ds(0, last * (PIECE // 128))
    parts = [
        pltpu.make_async_remote_copy(
            src_ref=ref, dst_ref=dst, send_sem=part_send.at[n], recv_sem=part_recv.at[n],
            device_id=other, device_id_type=MESH,
        )
        for n, (ref, dst, other) in enumerate(
            (
                (max_a, got.at[0], down),
                (max_c, got.at[1], up),
                (max_e.at[early], got.at[2, early], up_across),
            )
        )
    ]
    for copy in parts:
        copy.start()
    compare_e(last)
    work(ROWS * ROWS)
    answers = []
    for n, (s, d, f) in enumerate(LATE):
        answers.append(
            pltpu.make_async_remote_copy(
                src_ref=max_e.at[(N_MSG - PER + n) // 2], dst_ref=extra.at[n],
                send_sem=answer_send.at[n], recv_sem=answer_recv.at[n],
                device_id=routed(*moved(x, y, z, c, 1, True), s, d, f, -1), device_id_type=MESH,
            )
        )
    for copy in answers:
        copy.start()
    for copy in parts:
        copy.wait_recv()
    for n in range(ROWS // 128):
        best = jnp.maximum(max_b[n], jnp.maximum(got[0, n], got[1, n]))
        max_b[n] = jnp.maximum(best, got[2, n]) if n < last * (PIECE // 128) else best

    replies = []
    for j, (s, d, f) in enumerate(ORDER):
        if j == 0:
            continue
        replies.append(
            pltpu.make_async_remote_copy(
                src_ref=max_b.at[j // 2], dst_ref=table.at[j],
                send_sem=reply_send.at[j], recv_sem=reply_recv.at[j],
                device_id=routed(x, y, z, c, s, d, f, -1), device_id_type=MESH,
            )
        )
    for copy in replies:
        copy.start()
    table[0] = max_b[0]
    for copy in answers + replies:
        copy.wait_recv()

    values = jnp.concatenate(
        [table[j] if j < N_MSG - PER else jnp.maximum(table[j], extra[j - N_MSG + PER]) for j in range(N_MSG)], axis=0
    )
    high = values.astype(jnp.bfloat16)
    rest = values - high.astype(jnp.float32)
    mid = rest.astype(jnp.bfloat16)
    last = (rest - mid.astype(jnp.float32)).astype(jnp.bfloat16)
    choose = mine_f.astype(jnp.bfloat16)

    def taken(v):
        return lax.dot_general(v, choose, (((0,), (0,)), ((), ())), preferred_element_type=jnp.float32)

    lanes = taken(high) + taken(mid) + taken(last)
    want = (message & 1) * GROUP + rank
    at = lax.broadcasted_iota(jnp.int32, (128, count), 0)
    out_ref[...] = jnp.sum(jnp.where(at == want, lanes, 0.0), axis=0, keepdims=True)

    for j in range(N_MSG):
        if j:
            send(j).wait_send()
        spread(j, True).wait_send()
        spread(j, False).wait_send()
        relay(j).wait_send()
    for copy in parts + answers + replies:
        copy.wait_send()


def on_device(embed, dest, slot):
    count = embed.shape[0]
    width = embed.shape[1]
    vmem = pl.BlockSpec(memory_space=pltpu.VMEM)
    block = pltpu.VMEM((ROWS, width), jnp.bfloat16)
    low = pltpu.VMEM((1, ROWS), jnp.float32)
    best = pltpu.VMEM((ROWS // 128, 1, 128), jnp.float32)
    dma = pltpu.SemaphoreType.DMA
    out = pl.pallas_call(
        kernel,
        out_shape=jax.ShapeDtypeStruct((1, count), jnp.float32),
        in_specs=[pl.BlockSpec(memory_space=pl.ANY)] * 2,
        out_specs=vmem,
        scratch_shapes=[
            pltpu.VMEM((count, width), jnp.bfloat16), pltpu.VMEM((1, count), jnp.int32), dma((2,)),
            pltpu.VMEM((count, width), jnp.bfloat16), block, block, block, block, block, low, low, low, low,
            best, best, best, best,
            pltpu.VMEM((3, ROWS // 128, 1, 128), jnp.float32), pltpu.VMEM((N_MSG, 1, 128), jnp.float32),
            pltpu.VMEM((PER, 1, 128), jnp.float32),
        ]
        + [dma((N_MSG,))] * 8
        + [dma((3,)), dma((3,)), dma((N_MSG,)), dma((N_MSG,)), dma((PER,)), dma((PER,))],
        compiler_params=pltpu.CompilerParams(
            collective_id=0, has_side_effects=True, vmem_limit_bytes=60 * 2**20
        ),
        cost_estimate=pl.CostEstimate(flops=11 * 10**9, bytes_accessed=2 * 2**20, transcendentals=512),
    )(embed, dest.reshape(1, count))
    return out.reshape(count)


def solution(mesh):
    placed = (P(("grp", "blk"), None), P(("grp", "blk")), P(("grp", "blk")))
    return jax.shard_map(
        on_device, mesh=mesh, in_specs=placed, out_specs=P(("grp", "blk")), check_vma=False
    )
```

```python
import functools

import jax
import jax.numpy as jnp
from jax import lax
from jax.experimental import pallas as pl
from jax.experimental.pallas import tpu as pltpu
from jax.sharding import PartitionSpec as P

MESH = pl.DeviceIdType.MESH
BUDGET = 1024
LATER = 2
LAG = 4
GROUP = 64
N_MSG = 16
ROWS = GROUP * N_MSG
PIECE = 256
MARK = 4.0
LOW = -8.0

ORDER = [
    (0, 0, 0), (1, 0, 0), (0, 1, 0), (1, 1, 0), (0, 3, 0), (1, 3, 0), (0, 0, 1), (1, 0, 1),
    (0, 2, 0), (1, 2, 0), (0, 1, 1), (1, 1, 1), (0, 3, 1), (1, 3, 1), (0, 2, 1), (1, 2, 1),
]


PER = PIECE // GROUP
LATE = ORDER[N_MSG - PER :]


def place():
    g = lax.axis_index("grp")
    b = lax.axis_index("blk")
    x = ((b >> 2) << 1) + (g >> 3)
    return x, (g >> 1) & 3, b & 3, g & 1


def device(x, y, z, c):
    return (((x & 1) << 3) + (y << 1) + c, ((x >> 1) << 2) + z)


def flip(y, kind):
    return jnp.where(kind == 0, 3 - y, y + 1 - 2 * (y & 1))


def mate(y, kind):
    return flip(y, 1 - kind)


def routed(x, y, z, c, s, d, f, sign):
    return device(*end_of(x, y, z, c, s, d, f, sign))


def end_of(x, y, z, c, s, d, f, sign):
    here = c if s == 0 else 1 - c
    kind = here if sign == 1 else c
    step = sign * d
    yy = flip(y, kind) if f else y
    xx = jnp.where(kind == 0, (x + step) & 3, x)
    zz = jnp.where(kind == 0, z, (z + step) & 3)
    return xx, yy, zz, here


def moved(x, y, z, c, step, paired):
    yy = mate(y, c) if paired else y
    xx = jnp.where(c == 0, x, (x + step) & 3)
    zz = jnp.where(c == 0, (z + step) & 3, z)
    return xx, yy, zz, c


def ring(x, y, z, c, step, paired):
    return device(*moved(x, y, z, c, step, paired))


def nt(a, b):
    return lax.dot_general(a, b, (((1,), (1,)), ((), ())), preferred_element_type=jnp.float32)


def kernel(
    embed_hbm, dest_hbm, out_ref,
    embed_ref, dest_ref, load_sem, unit, pack, blk_b, blk_a, blk_c, blk_e, low_b, low_a, low_c, low_e,
    max_b, max_a, max_c, max_e, got, table, extra,
    pack_send, pack_recv, up_send, up_recv, down_send, down_recv, pair_send, pair_recv,
    part_send, part_recv, reply_send, reply_recv, answer_send, answer_recv,
):
    x, y, z, c = place()
    embed_in = pltpu.make_async_copy(embed_hbm, embed_ref, load_sem.at[0])
    dest_in = pltpu.make_async_copy(dest_hbm, dest_ref, load_sem.at[1])
    dest_in.start()
    embed_in.start()

    barrier = pltpu.get_barrier_semaphore()
    partners = []
    for s, d, f in ORDER[1:]:
        partners.append(routed(x, y, z, c, s, d, f, -1))
    for s, d, f in ORDER[1:]:
        if s == 1 and (d, f) != (0, 0):
            partners.append(routed(x, y, z, c, s, d, f, 1))
    up = ring(x, y, z, c, 1, False)
    down = ring(x, y, z, c, 3, False)
    across = ring(x, y, z, c, 0, True)
    up_across = ring(x, y, z, c, 1, True)
    down_across = ring(x, y, z, c, 3, True)
    partners += [up, down, across, down_across]
    for s, d, f in LATE:
        partners.append(ring(*end_of(x, y, z, c, s, d, f, 1), 3, True))
    for other in partners:
        pl.semaphore_signal(barrier, inc=1, device_id=other, device_id_type=MESH)

    dest_in.wait()
    dest = dest_ref[...]
    count = dest.shape[1]
    cluster = dest >> 3
    kind = cluster >> 3
    ring_at = (cluster >> 1) & 3
    pair_at = cluster & 1
    s_of = jnp.where(kind == c, 0, 1)
    d_of = (jnp.where(kind == 0, ring_at - x, ring_at - z)) & 3
    my_pair0 = y >> 1
    my_pair1 = ((y + 1) & 3) >> 1
    f_of = jnp.where(jnp.where(kind == 0, my_pair0, my_pair1) == pair_at, 0, 1)
    code = (d_of * 2 + f_of) * 2 + s_of
    message = jnp.zeros_like(code)
    for j, (s, d, f) in enumerate(ORDER):
        message = jnp.where(code == (d * 2 + f) * 2 + s, j, message)
    mine = lax.broadcasted_iota(jnp.int32, (N_MSG, count), 0) == message
    earlier = (
        lax.broadcasted_iota(jnp.int32, (count, count), 0)
        < lax.broadcasted_iota(jnp.int32, (count, count), 1)
    ).astype(jnp.float32).astype(jnp.bfloat16)
    mine_f = mine.astype(jnp.float32)
    before = jnp.dot(mine_f.astype(jnp.bfloat16), earlier, preferred_element_type=jnp.float32)
    rank = jnp.sum(before * mine_f, axis=0, keepdims=True).astype(jnp.int32)
    position = message * GROUP + rank

    embed_in.wait()
    wide = embed_ref[...].astype(jnp.float32)
    scale = lax.rsqrt(jnp.sum(wide * wide, axis=1, keepdims=True) + 1e-06)
    unit[...] = (wide * scale).astype(jnp.bfloat16)


    def send(j):
        s, d, f = ORDER[j]
        rows = pl.ds(j * GROUP, GROUP)
        return pltpu.make_async_remote_copy(
            src_ref=pack.at[pl.ds(j * GROUP, GROUP)], dst_ref=blk_b.at[rows],
            send_sem=pack_send.at[j], recv_sem=pack_recv.at[j],
            device_id=routed(x, y, z, c, s, d, f, 1), device_id_type=MESH,
        )

    def spread(j, upward):
        rows = pl.ds(j * GROUP, GROUP)
        return pltpu.make_async_remote_copy(
            src_ref=blk_b.at[rows], dst_ref=(blk_a if upward else blk_c).at[rows],
            send_sem=(up_send if upward else down_send).at[j],
            recv_sem=(up_recv if upward else down_recv).at[j],
            device_id=up if upward else down, device_id_type=MESH,
        )

    def relay(j):
        rows = pl.ds(j * GROUP, GROUP)
        return pltpu.make_async_remote_copy(
            src_ref=blk_c.at[rows], dst_ref=blk_e.at[rows],
            send_sem=pair_send.at[j], recv_sem=pair_recv.at[j],
            device_id=across, device_id_type=MESH,
        )

    part = 4
    size = ROWS // part
    for k in range(part):
        at = lax.broadcasted_iota(jnp.int32, (size, count), 0) + k * size
        pick = (at == position).astype(jnp.float32)
        rows = jnp.dot(pick.astype(jnp.bfloat16), unit[...], preferred_element_type=jnp.float32)
        empty = jnp.sum(pick, axis=1, keepdims=True) < 0.5
        lane = lax.broadcasted_iota(jnp.int32, (size, 128), 1)
        first = jnp.where(empty & (lane == 0), MARK, rows[:, :128])
        packed = jnp.concatenate([first, rows[:, 128:]], axis=1).astype(jnp.bfloat16)
        if k == 0:
            blk_b[pl.ds(0, GROUP), :] = packed[:GROUP]
            pack[pl.ds(GROUP, size - GROUP), :] = packed[GROUP:]
            pl.semaphore_wait(barrier, len(partners))
        else:
            pack[pl.ds(k * size, size), :] = packed
        for j in range(k * size // GROUP, (k + 1) * size // GROUP):
            if j == 0:
                spread(0, True).start()
                spread(0, False).start()
            else:
                send(j).start()

    ones = jnp.where(lax.broadcasted_iota(jnp.int32, (16, 128), 1) == 0, 1.0, 0.0).astype(jnp.bfloat16)
    blocks = {"a": (blk_a, low_a, max_a), "c": (blk_c, low_c, max_c), "e": (blk_e, low_e, max_e), "b": (blk_b, low_b, max_b)}
    here = {name: [] for name in blocks}

    def meets(one, i, two, j):
        if one == two:
            return one == "b"
        if "b" in (one, two):
            return "a" not in (one, two)
        if one == "e" or (one == "a" and two == "c"):
            i, j = j, i
        return i >= j

    def compare(name, q):
        block, low, left_max = blocks[name]
        rows = block[pl.ds(q * PIECE, PIECE), :]
        marks = nt(ones, rows[:, :128])[0:1]
        low[:, pl.ds(q * PIECE, PIECE)] = jnp.where(marks > 2.0, LOW, 0.0)
        here[name].append(q)
        spans = []
        for other in blocks:
            run = None
            once = name == "e" and other in ("a", "c")
            if once:
                spans.append((other, q * PIECE, PIECE))
            for k in range(ROWS // PIECE + 1):
                if k in here[other] and meets(name, q, other, k) and not (once and k == q):
                    run = k if run is None else run
                elif run is not None:
                    spans.append((other, run * PIECE, (k - run) * PIECE))
                    run = None
        for other, start, width in spans:
            for at in range(start, start + width, 2 * PIECE):
                wide = min(2 * PIECE, start + width - at)
                waiting.append((wide, functools.partial(product, name, q, other, at, wide)))

    def product(name, q, other, start, width):
        block, low, left_max = blocks[name]
        right, right_low, right_max = blocks[other]
        rows = block[pl.ds(q * PIECE, PIECE), :]
        tilt = jnp.where(rows[:, 0:1].astype(jnp.float32) > 2.0, LOW, 0.0)
        scores = nt(rows, right[pl.ds(start, width), :]) + tilt
        if other == name:
            at0 = lax.broadcasted_iota(jnp.int32, scores.shape, 0) + q * PIECE
            at1 = lax.broadcasted_iota(jnp.int32, scores.shape, 1) + start
            scores = jnp.where(at0 == at1, LOW, scores)
        if not (name == "e" and other in ("a", "c") and start == q * PIECE):
            tops = jnp.max(scores, axis=0, keepdims=True)
            for n in range(width // 128):
                at = start // 128 + n
                right_max[at] = jnp.maximum(right_max[at], tops[:, n * 128 : (n + 1) * 128])
        scores = scores + right_low[:, pl.ds(start, width)]
        best = None
        for n in range(width // 128):
            tile = scores[:, n * 128 : (n + 1) * 128]
            best = tile if best is None else jnp.maximum(best, tile)
        for n in range(PIECE // 128):
            turned = best[n * 128 : (n + 1) * 128, :].T
            at = q * (PIECE // 128) + n
            left_max[at] = jnp.maximum(left_max[at], jnp.max(turned, axis=0, keepdims=True))

    def work(budget):
        while waiting and budget > 0:
            wide, step = waiting.pop(0)
            step()
            budget -= wide

    waiting = []
    last = ROWS // PIECE - 1

    def of_piece(q):
        return range(q * PER, (q + 1) * PER)

    def compare_e(q):
        for j in of_piece(q):
            relay(j).wait_recv()
        compare("e", q)

    for ref in (max_b, max_a, max_c, max_e):
        ref[...] = jnp.full(ref.shape, LOW, jnp.float32)
    for step in range(N_MSG + LAG):
        j, k = step, step - LAG
        if 0 < j < N_MSG:
            send(j).wait_recv()
            spread(j, True).start()
            spread(j, False).start()
        if k >= 0:
            spread(k, False).wait_recv()
            relay(k).start()
        if j < N_MSG and j % PER == PER - 1:
            compare("b", j // PER)
        if k >= 0 and k % PER == PER - 1:
            compare("c", k // PER)
            for n in of_piece(k // PER):
                spread(n, True).wait_recv()
            compare("a", k // PER)
        if k >= PER and (k - LATER) % PER == PER - 1 and (k - LATER) // PER < last:
            compare_e((k - LATER) // PER)
        if step < N_MSG + LAG - 1:
            work(BUDGET)
    work(ROWS * ROWS)

    early = pl.ds(0, last * (PIECE // 128))
    parts = [
        pltpu.make_async_remote_copy(
            src_ref=ref, dst_ref=dst, send_sem=part_send.at[n], recv_sem=part_recv.at[n],
            device_id=other, device_id_type=MESH,
        )
        for n, (ref, dst, other) in enumerate(
            (
                (max_a, got.at[0], down),
                (max_c, got.at[1], up),
                (max_e.at[early], got.at[2, early], up_across),
            )
        )
    ]
    for copy in parts:
        copy.start()
    compare_e(last)
    work(ROWS * ROWS)
    answers = []
    for n, (s, d, f) in enumerate(LATE):
        answers.append(
            pltpu.make_async_remote_copy(
                src_ref=max_e.at[(N_MSG - PER + n) // 2], dst_ref=extra.at[n],
                send_sem=answer_send.at[n], recv_sem=answer_recv.at[n],
                device_id=routed(*moved(x, y, z, c, 1, True), s, d, f, -1), device_id_type=MESH,
            )
        )
    for copy in answers:
        copy.start()
    for copy in parts:
        copy.wait_recv()
    for n in range(ROWS // 128):
        best = jnp.maximum(max_b[n], jnp.maximum(got[0, n], got[1, n]))
        max_b[n] = jnp.maximum(best, got[2, n]) if n < last * (PIECE // 128) else best

    replies = []
    for j, (s, d, f) in enumerate(ORDER):
        if j == 0:
            continue
        replies.append(
            pltpu.make_async_remote_copy(
                src_ref=max_b.at[j // 2], dst_ref=table.at[j],
                send_sem=reply_send.at[j], recv_sem=reply_recv.at[j],
                device_id=routed(x, y, z, c, s, d, f, -1), device_id_type=MESH,
            )
        )
    for copy in replies:
        copy.start()
    table[0] = max_b[0]
    for copy in answers + replies:
        copy.wait_recv()

    values = jnp.concatenate(
        [table[j] if j < N_MSG - PER else jnp.maximum(table[j], extra[j - N_MSG + PER]) for j in range(N_MSG)], axis=0
    )
    high = values.astype(jnp.bfloat16)
    rest = values - high.astype(jnp.float32)
    mid = rest.astype(jnp.bfloat16)
    last = (rest - mid.astype(jnp.float32)).astype(jnp.bfloat16)
    choose = mine_f.astype(jnp.bfloat16)

    def taken(v):
        return lax.dot_general(v, choose, (((0,), (0,)), ((), ())), preferred_element_type=jnp.float32)

    lanes = taken(high) + taken(mid) + taken(last)
    want = (message & 1) * GROUP + rank
    at = lax.broadcasted_iota(jnp.int32, (128, count), 0)
    out_ref[...] = jnp.sum(jnp.where(at == want, lanes, 0.0), axis=0, keepdims=True)

    for j in range(N_MSG):
        if j:
            send(j).wait_send()
        spread(j, True).wait_send()
        spread(j, False).wait_send()
        relay(j).wait_send()
    for copy in parts + answers + replies:
        copy.wait_send()


def on_device(embed, dest, slot):
    count = embed.shape[0]
    width = embed.shape[1]
    vmem = pl.BlockSpec(memory_space=pltpu.VMEM)
    block = pltpu.VMEM((ROWS, width), jnp.bfloat16)
    low = pltpu.VMEM((1, ROWS), jnp.float32)
    best = pltpu.VMEM((ROWS // 128, 1, 128), jnp.float32)
    dma = pltpu.SemaphoreType.DMA
    out = pl.pallas_call(
        kernel,
        out_shape=pltpu.VMEM((1, count), jnp.float32),
        in_specs=[pl.BlockSpec(memory_space=pl.ANY)] * 2,
        out_specs=vmem,
        scratch_shapes=[
            pltpu.VMEM((count, width), jnp.bfloat16), pltpu.VMEM((1, count), jnp.int32), dma((2,)),
            pltpu.VMEM((count, width), jnp.bfloat16), block, block, block, block, block, low, low, low, low,
            best, best, best, best,
            pltpu.VMEM((3, ROWS // 128, 1, 128), jnp.float32), pltpu.VMEM((N_MSG, 1, 128), jnp.float32),
            pltpu.VMEM((PER, 1, 128), jnp.float32),
        ]
        + [dma((N_MSG,))] * 8
        + [dma((3,)), dma((3,)), dma((N_MSG,)), dma((N_MSG,)), dma((PER,)), dma((PER,))],
        compiler_params=pltpu.CompilerParams(
            collective_id=0, has_side_effects=True, vmem_limit_bytes=60 * 2**20
        ),
        cost_estimate=pl.CostEstimate(flops=11 * 10**9, bytes_accessed=2 * 2**20, transcendentals=512),
    )(embed, dest.reshape(1, count))
    return out.reshape(count)


def solution(mesh):
    placed = (P(("grp", "blk"), None), P(("grp", "blk")), P(("grp", "blk")))
    return jax.shard_map(
        on_device, mesh=mesh, in_specs=placed, out_specs=P(("grp", "blk")), check_vma=False
    )
```

```python
import functools

import jax
import jax.numpy as jnp
from jax import lax
from jax.experimental import pallas as pl
from jax.experimental.pallas import tpu as pltpu
from jax.sharding import PartitionSpec as P

MESH = pl.DeviceIdType.MESH
BUDGET = 1024
LATER = 3
LAG = 4
GROUP = 64
N_MSG = 16
ROWS = GROUP * N_MSG
PIECE = 256
MARK = 4.0
LOW = -8.0

ORDER = [
    (0, 0, 0), (1, 0, 0), (0, 1, 0), (1, 1, 0), (0, 3, 0), (1, 3, 0), (0, 0, 1), (1, 0, 1),
    (0, 2, 0), (1, 2, 0), (0, 1, 1), (1, 1, 1), (0, 3, 1), (1, 3, 1), (0, 2, 1), (1, 2, 1),
]


PER = PIECE // GROUP
LATE = ORDER[N_MSG - PER :]


def place():
    g = lax.axis_index("grp")
    b = lax.axis_index("blk")
    x = ((b >> 2) << 1) + (g >> 3)
    return x, (g >> 1) & 3, b & 3, g & 1


def device(x, y, z, c):
    return (((x & 1) << 3) + (y << 1) + c, ((x >> 1) << 2) + z)


def flip(y, kind):
    return jnp.where(kind == 0, 3 - y, y + 1 - 2 * (y & 1))


def mate(y, kind):
    return flip(y, 1 - kind)


def routed(x, y, z, c, s, d, f, sign):
    return device(*end_of(x, y, z, c, s, d, f, sign))


def end_of(x, y, z, c, s, d, f, sign):
    here = c if s == 0 else 1 - c
    kind = here if sign == 1 else c
    step = sign * d
    yy = flip(y, kind) if f else y
    xx = jnp.where(kind == 0, (x + step) & 3, x)
    zz = jnp.where(kind == 0, z, (z + step) & 3)
    return xx, yy, zz, here


def moved(x, y, z, c, step, paired):
    yy = mate(y, c) if paired else y
    xx = jnp.where(c == 0, x, (x + step) & 3)
    zz = jnp.where(c == 0, (z + step) & 3, z)
    return xx, yy, zz, c


def ring(x, y, z, c, step, paired):
    return device(*moved(x, y, z, c, step, paired))


def nt(a, b):
    return lax.dot_general(a, b, (((1,), (1,)), ((), ())), preferred_element_type=jnp.float32)


def kernel(
    embed_hbm, dest_hbm, out_ref,
    embed_ref, dest_ref, load_sem, unit, pack, blk_b, blk_a, blk_c, blk_e, low_b, low_a, low_c, low_e,
    max_b, max_a, max_c, max_e, got, table, extra,
    pack_send, pack_recv, up_send, up_recv, down_send, down_recv, pair_send, pair_recv,
    part_send, part_recv, reply_send, reply_recv, answer_send, answer_recv,
):
    x, y, z, c = place()
    embed_in = pltpu.make_async_copy(embed_hbm, embed_ref, load_sem.at[0])
    dest_in = pltpu.make_async_copy(dest_hbm, dest_ref, load_sem.at[1])
    dest_in.start()
    embed_in.start()

    barrier = pltpu.get_barrier_semaphore()
    partners = []
    for s, d, f in ORDER[1:]:
        partners.append(routed(x, y, z, c, s, d, f, -1))
    for s, d, f in ORDER[1:]:
        if s == 1 and (d, f) != (0, 0):
            partners.append(routed(x, y, z, c, s, d, f, 1))
    up = ring(x, y, z, c, 1, False)
    down = ring(x, y, z, c, 3, False)
    across = ring(x, y, z, c, 0, True)
    up_across = ring(x, y, z, c, 1, True)
    down_across = ring(x, y, z, c, 3, True)
    partners += [up, down, across, down_across]
    for s, d, f in LATE:
        partners.append(ring(*end_of(x, y, z, c, s, d, f, 1), 3, True))
    for other in partners:
        pl.semaphore_signal(barrier, inc=1, device_id=other, device_id_type=MESH)

    dest_in.wait()
    dest = dest_ref[...]
    count = dest.shape[1]
    cluster = dest >> 3
    kind = cluster >> 3
    ring_at = (cluster >> 1) & 3
    pair_at = cluster & 1
    s_of = jnp.where(kind == c, 0, 1)
    d_of = (jnp.where(kind == 0, ring_at - x, ring_at - z)) & 3
    my_pair0 = y >> 1
    my_pair1 = ((y + 1) & 3) >> 1
    f_of = jnp.where(jnp.where(kind == 0, my_pair0, my_pair1) == pair_at, 0, 1)
    code = (d_of * 2 + f_of) * 2 + s_of
    message = jnp.zeros_like(code)
    for j, (s, d, f) in enumerate(ORDER):
        message = jnp.where(code == (d * 2 + f) * 2 + s, j, message)
    mine = lax.broadcasted_iota(jnp.int32, (N_MSG, count), 0) == message
    earlier = (
        lax.broadcasted_iota(jnp.int32, (count, count), 0)
        < lax.broadcasted_iota(jnp.int32, (count, count), 1)
    ).astype(jnp.float32).astype(jnp.bfloat16)
    mine_f = mine.astype(jnp.float32)
    before = jnp.dot(mine_f.astype(jnp.bfloat16), earlier, preferred_element_type=jnp.float32)
    rank = jnp.sum(before * mine_f, axis=0, keepdims=True).astype(jnp.int32)
    position = message * GROUP + rank

    embed_in.wait()
    wide = embed_ref[...].astype(jnp.float32)
    scale = lax.rsqrt(jnp.sum(wide * wide, axis=1, keepdims=True) + 1e-06)
    unit[...] = (wide * scale).astype(jnp.bfloat16)


    def send(j):
        s, d, f = ORDER[j]
        rows = pl.ds(j * GROUP, GROUP)
        return pltpu.make_async_remote_copy(
            src_ref=pack.at[pl.ds(j * GROUP, GROUP)], dst_ref=blk_b.at[rows],
            send_sem=pack_send.at[j], recv_sem=pack_recv.at[j],
            device_id=routed(x, y, z, c, s, d, f, 1), device_id_type=MESH,
        )

    def spread(j, upward):
        rows = pl.ds(j * GROUP, GROUP)
        return pltpu.make_async_remote_copy(
            src_ref=blk_b.at[rows], dst_ref=(blk_a if upward else blk_c).at[rows],
            send_sem=(up_send if upward else down_send).at[j],
            recv_sem=(up_recv if upward else down_recv).at[j],
            device_id=up if upward else down, device_id_type=MESH,
        )

    def relay(j):
        rows = pl.ds(j * GROUP, GROUP)
        return pltpu.make_async_remote_copy(
            src_ref=blk_c.at[rows], dst_ref=blk_e.at[rows],
            send_sem=pair_send.at[j], recv_sem=pair_recv.at[j],
            device_id=across, device_id_type=MESH,
        )

    part = 4
    size = ROWS // part
    for k in range(part):
        at = lax.broadcasted_iota(jnp.int32, (size, count), 0) + k * size
        pick = (at == position).astype(jnp.float32)
        rows = jnp.dot(pick.astype(jnp.bfloat16), unit[...], preferred_element_type=jnp.float32)
        empty = jnp.sum(pick, axis=1, keepdims=True) < 0.5
        lane = lax.broadcasted_iota(jnp.int32, (size, 128), 1)
        first = jnp.where(empty & (lane == 0), MARK, rows[:, :128])
        packed = jnp.concatenate([first, rows[:, 128:]], axis=1).astype(jnp.bfloat16)
        if k == 0:
            blk_b[pl.ds(0, GROUP), :] = packed[:GROUP]
            pack[pl.ds(GROUP, size - GROUP), :] = packed[GROUP:]
            pl.semaphore_wait(barrier, len(partners))
        else:
            pack[pl.ds(k * size, size), :] = packed
        for j in range(k * size // GROUP, (k + 1) * size // GROUP):
            if j == 0:
                spread(0, True).start()
                spread(0, False).start()
            else:
                send(j).start()

    ones = jnp.where(lax.broadcasted_iota(jnp.int32, (16, 128), 1) == 0, 1.0, 0.0).astype(jnp.bfloat16)
    blocks = {"a": (blk_a, low_a, max_a), "c": (blk_c, low_c, max_c), "e": (blk_e, low_e, max_e), "b": (blk_b, low_b, max_b)}
    here = {name: [] for name in blocks}

    def meets(one, i, two, j):
        if one == two:
            return one == "b"
        if "b" in (one, two):
            return "a" not in (one, two)
        if one == "e" or (one == "a" and two == "c"):
            i, j = j, i
        return i >= j

    def compare(name, q):
        block, low, left_max = blocks[name]
        rows = block[pl.ds(q * PIECE, PIECE), :]
        marks = nt(ones, rows[:, :128])[0:1]
        low[:, pl.ds(q * PIECE, PIECE)] = jnp.where(marks > 2.0, LOW, 0.0)
        here[name].append(q)
        spans = []
        for other in blocks:
            run = None
            once = name == "e" and other in ("a", "c")
            if once:
                spans.append((other, q * PIECE, PIECE))
            for k in range(ROWS // PIECE + 1):
                if k in here[other] and meets(name, q, other, k) and not (once and k == q):
                    run = k if run is None else run
                elif run is not None:
                    spans.append((other, run * PIECE, (k - run) * PIECE))
                    run = None
        for other, start, width in spans:
            for at in range(start, start + width, 2 * PIECE):
                wide = min(2 * PIECE, start + width - at)
                waiting.append((wide, functools.partial(product, name, q, other, at, wide)))

    def product(name, q, other, start, width):
        block, low, left_max = blocks[name]
        right, right_low, right_max = blocks[other]
        rows = block[pl.ds(q * PIECE, PIECE), :]
        tilt = jnp.where(rows[:, 0:1].astype(jnp.float32) > 2.0, LOW, 0.0)
        scores = nt(rows, right[pl.ds(start, width), :]) + tilt
        if other == name:
            at0 = lax.broadcasted_iota(jnp.int32, scores.shape, 0) + q * PIECE
            at1 = lax.broadcasted_iota(jnp.int32, scores.shape, 1) + start
            scores = jnp.where(at0 == at1, LOW, scores)
        if not (name == "e" and other in ("a", "c") and start == q * PIECE):
            tops = jnp.max(scores, axis=0, keepdims=True)
            for n in range(width // 128):
                at = start // 128 + n
                right_max[at] = jnp.maximum(right_max[at], tops[:, n * 128 : (n + 1) * 128])
        scores = scores + right_low[:, pl.ds(start, width)]
        best = None
        for n in range(width // 128):
            tile = scores[:, n * 128 : (n + 1) * 128]
            best = tile if best is None else jnp.maximum(best, tile)
        for n in range(PIECE // 128):
            turned = best[n * 128 : (n + 1) * 128, :].T
            at = q * (PIECE // 128) + n
            left_max[at] = jnp.maximum(left_max[at], jnp.max(turned, axis=0, keepdims=True))

    def work(budget):
        while waiting and budget > 0:
            wide, step = waiting.pop(0)
            step()
            budget -= wide

    waiting = []
    last = ROWS // PIECE - 1

    def of_piece(q):
        return range(q * PER, (q + 1) * PER)

    def compare_e(q):
        for j in of_piece(q):
            relay(j).wait_recv()
        compare("e", q)

    for ref in (max_b, max_a, max_c, max_e):
        ref[...] = jnp.full(ref.shape, LOW, jnp.float32)
    for step in range(N_MSG + LAG):
        j, k = step, step - LAG
        if 0 < j < N_MSG:
            send(j).wait_recv()
            spread(j, True).start()
            spread(j, False).start()
        if k >= 0:
            spread(k, False).wait_recv()
            relay(k).start()
        if j < N_MSG and j % PER == PER - 1:
            compare("b", j // PER)
        if k >= 0 and k % PER == PER - 1:
            compare("c", k // PER)
            for n in of_piece(k // PER):
                spread(n, True).wait_recv()
            compare("a", k // PER)
        if k >= PER and (k - LATER) % PER == PER - 1 and (k - LATER) // PER < last:
            compare_e((k - LATER) // PER)
        if step < N_MSG + LAG - 1:
            work(BUDGET)
    work(ROWS * ROWS)

    early = pl.ds(0, last * (PIECE // 128))
    parts = [
        pltpu.make_async_remote_copy(
            src_ref=ref, dst_ref=dst, send_sem=part_send.at[n], recv_sem=part_recv.at[n],
            device_id=other, device_id_type=MESH,
        )
        for n, (ref, dst, other) in enumerate(
            (
                (max_a, got.at[0], down),
                (max_c, got.at[1], up),
                (max_e.at[early], got.at[2, early], up_across),
            )
        )
    ]
    for copy in parts:
        copy.start()
    compare_e(last)
    work(ROWS * ROWS)
    answers = []
    for n, (s, d, f) in enumerate(LATE):
        answers.append(
            pltpu.make_async_remote_copy(
                src_ref=max_e.at[(N_MSG - PER + n) // 2], dst_ref=extra.at[n],
                send_sem=answer_send.at[n], recv_sem=answer_recv.at[n],
                device_id=routed(*moved(x, y, z, c, 1, True), s, d, f, -1), device_id_type=MESH,
            )
        )
    for copy in answers:
        copy.start()
    for copy in parts:
        copy.wait_recv()
    for n in range(ROWS // 128):
        best = jnp.maximum(max_b[n], jnp.maximum(got[0, n], got[1, n]))
        max_b[n] = jnp.maximum(best, got[2, n]) if n < last * (PIECE // 128) else best

    replies = []
    for j, (s, d, f) in enumerate(ORDER):
        if j == 0:
            continue
        replies.append(
            pltpu.make_async_remote_copy(
                src_ref=max_b.at[j // 2], dst_ref=table.at[j],
                send_sem=reply_send.at[j], recv_sem=reply_recv.at[j],
                device_id=routed(x, y, z, c, s, d, f, -1), device_id_type=MESH,
            )
        )
    for copy in replies:
        copy.start()
    table[0] = max_b[0]
    for copy in answers + replies:
        copy.wait_recv()

    values = jnp.concatenate(
        [table[j] if j < N_MSG - PER else jnp.maximum(table[j], extra[j - N_MSG + PER]) for j in range(N_MSG)], axis=0
    )
    high = values.astype(jnp.bfloat16)
    rest = values - high.astype(jnp.float32)
    mid = rest.astype(jnp.bfloat16)
    last = (rest - mid.astype(jnp.float32)).astype(jnp.bfloat16)
    choose = mine_f.astype(jnp.bfloat16)

    def taken(v):
        return lax.dot_general(v, choose, (((0,), (0,)), ((), ())), preferred_element_type=jnp.float32)

    lanes = taken(high) + taken(mid) + taken(last)
    want = (message & 1) * GROUP + rank
    at = lax.broadcasted_iota(jnp.int32, (128, count), 0)
    out_ref[...] = jnp.sum(jnp.where(at == want, lanes, 0.0), axis=0, keepdims=True)

    for j in range(N_MSG):
        if j:
            send(j).wait_send()
        spread(j, True).wait_send()
        spread(j, False).wait_send()
        relay(j).wait_send()
    for copy in parts + answers + replies:
        copy.wait_send()


def on_device(embed, dest, slot):
    count = embed.shape[0]
    width = embed.shape[1]
    vmem = pl.BlockSpec(memory_space=pltpu.VMEM)
    block = pltpu.VMEM((ROWS, width), jnp.bfloat16)
    low = pltpu.VMEM((1, ROWS), jnp.float32)
    best = pltpu.VMEM((ROWS // 128, 1, 128), jnp.float32)
    dma = pltpu.SemaphoreType.DMA
    out = pl.pallas_call(
        kernel,
        out_shape=pltpu.VMEM((1, count), jnp.float32),
        in_specs=[pl.BlockSpec(memory_space=pl.ANY)] * 2,
        out_specs=vmem,
        scratch_shapes=[
            pltpu.VMEM((count, width), jnp.bfloat16), pltpu.VMEM((1, count), jnp.int32), dma((2,)),
            pltpu.VMEM((count, width), jnp.bfloat16), block, block, block, block, block, low, low, low, low,
            best, best, best, best,
            pltpu.VMEM((3, ROWS // 128, 1, 128), jnp.float32), pltpu.VMEM((N_MSG, 1, 128), jnp.float32),
            pltpu.VMEM((PER, 1, 128), jnp.float32),
        ]
        + [dma((N_MSG,))] * 8
        + [dma((3,)), dma((3,)), dma((N_MSG,)), dma((N_MSG,)), dma((PER,)), dma((PER,))],
        compiler_params=pltpu.CompilerParams(
            collective_id=0, has_side_effects=True, vmem_limit_bytes=60 * 2**20
        ),
        cost_estimate=pl.CostEstimate(flops=11 * 10**9, bytes_accessed=2 * 2**20, transcendentals=512),
    )(embed, dest.reshape(1, count))
    return out.reshape(count)


def solution(mesh):
    placed = (P(("grp", "blk"), None), P(("grp", "blk")), P(("grp", "blk")))
    return jax.shard_map(
        on_device, mesh=mesh, in_specs=placed, out_specs=P(("grp", "blk")), check_vma=False
    )
```
